256 devices in a mesh: branch: 32 (over y_hi, z, core), tensor: 8 (over y_lo, x).
Axes of the slice: x: 4, y: 4 (y_hi: 2, y_lo: 2; y = y_hi * 2 + y_lo), z: 8, core: 2. Of those that a mesh axis runs over, the one named last changes fastest.
Arguments:
- queries: bfloat16 [256, 4, 8192], P('branch', None, 'tensor'), may hold values from -72 to 72, as said below
- new_keys: bfloat16 [256, 4, 1024], P('branch', None, 'tensor'), may hold values from -12 to 12
- new_values: bfloat16 [256, 4, 1024], P('branch', None, 'tensor'), may hold values from -6 to 6
- pool_keys: bfloat16 [3072, 16, 1024], P('branch', None, 'tensor'), may hold values from -12 to 12
- pool_values: bfloat16 [3072, 16, 1024], P('branch', None, 'tensor'), may hold values from -6 to 6
- out_weight: bfloat16 [8192, 4096], P('tensor'), may hold values from -0.0625 to 0.0625
- page_table: int32 [32, 1024], replicated, may hold values from 0 to 3071, as said below
- prefix_len: int32 [32], replicated, may hold values from 8192 to 16384, as said below
- parent: int32 [256], P('branch'), may hold values from 0 to 31, as said below
- finished: int32 [256, 4], P('branch'), may hold values from 0 to 1, as said below
Outputs:
- projected: float32 [256, 4, 4096], P('branch', None, 'tensor')
The draws below stay inside these ranges and needn't reach their ends.
Inputs may be any that keep to these rules, and one draw needn't show every extreme that they name: Each row queries[c, s] is either drawn independently of the keys, or, for some pool page p and slot r and some factor f > 1, query head h equals f times key head h // 8 of pool_keys[p, r] for every h. `page_table`: no pool page appears twice in one node's path; all paths begin with the same run of pages, nodes 4 k to 4 k + 3 share the next run, and each path ends in a run of pages that no other path holds. `prefix_len`: some node has the full 1024 * 16 tokens. Every node is the parent of exactly 8 children. Once a child has finished it stays finished at later steps.
All inputs are finite; a program needn't handle non-finite values.
Results may differ from the reference program's by a relative error of at most 0.0075.
Values may be sent and summed in bfloat16 or wider, within the bound.
No kernel may reach another device: no remote copies, remote signals or barrier semaphores. Data moves between devices by JAX's collectives and lax.ppermute only.
A program may use at most 128 MiB of HBM per device.

```python
import jax
import jax.numpy as jnp
from jax import lax

D = 4096
QH = 64
KVH = 8
HD = 128
PAGE = 16
FORK = 8
STEPS = 4
PATH_PAGES = 1024
CHILDREN = 256
NODES = 32
POOL = 3072


def shared_keys(key):
    return jnp.clip(jax.random.normal(key, (POOL, PAGE, KVH * HD), jnp.float32), -6.0, 6.0)


def tree_table(key):
    key = jax.random.fold_in(key, 11)
    own = max(1, min(PATH_PAGES // 8, POOL // (8 * NODES)))
    groups = (NODES + 3) // 4
    root = PATH_PAGES - 2 * own
    order = jax.random.permutation(key, POOL).astype(jnp.int32)
    places = jnp.arange(POOL, dtype=jnp.int32)
    first = order[0]
    order = jnp.where(order == POOL - 1, first, jnp.where(places == 0, POOL - 1, order)).astype(jnp.int32)
    second = order[1]
    order = jnp.where(order == 0, second, jnp.where(places == 1, 0, order)).astype(jnp.int32)
    root_pages = order[:root]
    shared_runs = order[root:root + groups * own].reshape(groups, own)
    own_runs = order[root + groups * own:root + groups * own + NODES * own].reshape(NODES, own)
    nodes = jnp.arange(NODES, dtype=jnp.int32)
    table = jnp.concatenate([jnp.broadcast_to(root_pages[None, :], (NODES, root)), shared_runs[nodes // 4], own_runs], axis=1)
    return table.astype(jnp.int32)


def draw_page_table(key, part):
    return tree_table(key)


def draw_pool_keys(key, part):
    base = shared_keys(key)
    return (2.0 * base).astype(jnp.bfloat16)


def draw_queries(key, part):
    key = jax.random.fold_in(key, 2)
    drawn = jnp.clip(jax.random.normal(key, (CHILDREN, STEPS, QH * HD), jnp.float32), -6.0, 6.0)
    return drawn.astype(jnp.bfloat16)


def draw_prefix_len(key, part):
    key = jax.random.fold_in(key, 3)
    length_key, index_key = jax.random.split(key)
    most = PATH_PAGES * PAGE
    lengths = jax.random.randint(length_key, (NODES,), most // 2, most + 1)
    where_full = jax.random.randint(index_key, (), 0, NODES)
    return lengths.at[where_full].set(most).astype(jnp.int32)


def draw_parent(key, part):
    key = jax.random.fold_in(key, 4)
    return (jax.random.permutation(key, CHILDREN).astype(jnp.int32) // FORK).astype(jnp.int32)


def draw_finished(key, part):
    key = jax.random.fold_in(key, 6)
    stop = jax.random.randint(key, (CHILDREN,), 0, STEPS + 2)
    return (jnp.arange(STEPS, dtype=jnp.int32)[None, :] >= stop[:, None]).astype(jnp.int32)


def shard_levels(own_key, shape, cuts, least, largest):
    gain = 1.0
    for position, blocks in cuts:
        steps = jax.random.uniform(jax.random.fold_in(jax.random.fold_in(own_key, 6), position), (blocks,), jnp.float32, least / len(cuts), largest / len(cuts))
        gain = gain * jnp.repeat(jnp.exp(steps), shape[position] // blocks).reshape((-1,) + (1,) * (len(shape) - 1 - position))
    return gain


def gaussian(stream_key, shape, width, reach, cuts=(), kind=jnp.bfloat16):
    values = jax.random.normal(stream_key, shape, jnp.float32) * width
    if len(cuts) > 0:
        values = shard_levels(stream_key, shape, cuts, -0.22, 0.18) * values
    return jnp.clip(values, min=-reach, max=reach).astype(kind)


def setup_inputs(seed: int = 0) -> dict:
    streams_of = jax.random.split(jax.random.key(seed), 11)
    queries = draw_queries(jax.random.fold_in(streams_of[10], 71), 0)
    new_keys = gaussian(streams_of[1], (CHILDREN, STEPS, KVH * HD), 2.0, 12.0, ((0, 32), (2, 8)))
    new_values = gaussian(streams_of[2], (CHILDREN, STEPS, KVH * HD), 1.0, 6.0, ((0, 32), (2, 8)))
    pool_keys = draw_pool_keys(jax.random.fold_in(streams_of[10], 71), 0)
    pool_values = gaussian(streams_of[4], (POOL, PAGE, KVH * HD), 1.0, 6.0, ((0, 32), (2, 8)))
    out_weight = gaussian(streams_of[5], (QH * HD, D), (QH * HD) ** -0.5, 0.0625, ((0, 8),))
    page_table = draw_page_table(jax.random.fold_in(streams_of[10], 71), 0)
    prefix_len = draw_prefix_len(jax.random.fold_in(streams_of[10], 71), 0)
    parent = draw_parent(jax.random.fold_in(streams_of[10], 71), 0)
    finished = draw_finished(jax.random.fold_in(streams_of[10], 71), 0)
    return dict(queries=queries, new_keys=new_keys, new_values=new_values, pool_keys=pool_keys, pool_values=pool_values, out_weight=out_weight, page_table=page_table, prefix_len=prefix_len, parent=parent, finished=finished)


NEGATIVE = -1.0e30


def reference(queries, new_keys, new_values, pool_keys, pool_values, out_weight, page_table, prefix_len, parent, finished):
    group = QH // KVH
    scale = HD ** -0.5
    order = jnp.arange(STEPS, dtype=jnp.int32)
    places = jnp.arange(PATH_PAGES * PAGE, dtype=jnp.int32)

    def one_child(inputs):
        query, own_keys, own_values, node, gone = inputs
        pages = page_table[node]
        keys = jnp.take(pool_keys, pages, axis=0).reshape(PATH_PAGES * PAGE, KVH, HD).astype(jnp.float32)
        values = jnp.take(pool_values, pages, axis=0).reshape(PATH_PAGES * PAGE, KVH, HD).astype(jnp.float32)
        inside = places < prefix_len[node]
        rows = query.reshape(STEPS, KVH, group, HD).astype(jnp.float32)
        path_scores = jnp.einsum("skgd,tkd->skgt", rows, keys) * scale
        path_scores = jnp.where(inside, path_scores, NEGATIVE)
        alive = 1 - gone
        allowed = (order[None, :] <= order[:, None]) & (alive[None, :] > 0)
        allowed = allowed[:, None, None, :]
        own_k = own_keys.reshape(STEPS, KVH, HD).astype(jnp.float32)
        own_v = own_values.reshape(STEPS, KVH, HD).astype(jnp.float32)
        own_scores = jnp.einsum("skgd,jkd->skgj", rows, own_k) * scale
        own_scores = jnp.where(allowed, own_scores, NEGATIVE)
        top = jnp.maximum(jnp.max(path_scores, axis=-1), jnp.max(own_scores, axis=-1))
        path_p = jnp.where(inside, jnp.exp(path_scores - top[..., None]), 0.0)
        own_p = jnp.where(allowed, jnp.exp(own_scores - top[..., None]), 0.0)
        total = jnp.sum(path_p, axis=-1) + jnp.sum(own_p, axis=-1)
        path_w = lax.optimization_barrier(path_p.astype(jnp.bfloat16)).astype(jnp.float32)
        own_w = lax.optimization_barrier(own_p.astype(jnp.bfloat16)).astype(jnp.float32)
        summed = jnp.einsum("skgt,tkd->skgd", path_w, values) + jnp.einsum("skgj,jkd->skgd", own_w, own_v)
        attended = (summed / total[..., None]).astype(jnp.bfloat16)
        out = jnp.dot(attended.reshape(STEPS, QH * HD), out_weight, preferred_element_type=jnp.float32)
        return out * alive[:, None].astype(jnp.float32)

    return lax.map(one_child, (queries, new_keys, new_values, parent, finished))
```

```python
import functools

import jax
import jax.numpy as jnp
from jax import lax
from jax.experimental import pallas as pl
from jax.experimental.pallas import tpu as pltpu
from jax.sharding import Mesh, PartitionSpec as P

HD = 128
PAGE = 16
PAGES_DEV = 96
GROUPS = 4
RING = 8
ROWS = 256
HEADS = 8
CS = 32
TILE = 1024
BIG = 2.0**100
LOW = -3.0e38
C2 = HD**-0.5 * 1.4426950408889634
MIB = 1024 * 1024


def mask_kernel(first_ref, table_ref, left_ref, count_ref, bias_ref):
    left = left_ref[...]
    for block in range(GROUPS):
        first = first_ref[block]

        def one_page(page, carry, block=block, first=first):
            hit = jnp.where(table_ref[...] == first + page, left, 0)
            count_ref[pl.ds(block * PAGES_DEV + page, 1), :] = jnp.sum(hit, axis=0, keepdims=True)
            return carry

        lax.fori_loop(0, PAGES_DEV, one_page, 0, unroll=8)
    part = count_ref[...]
    part = part + pltpu.roll(part, 64, 1)
    count_ref[...] = part + pltpu.roll(part, 32, 1)
    token = lax.broadcasted_iota(jnp.int32, (PAGE, HD), 0)

    def one_bias(page, carry):
        held = jnp.broadcast_to(count_ref[pl.ds(page, 1), :], (PAGE, HD))
        bias = jnp.where(token >= held, -BIG, 0.0).astype(jnp.bfloat16)
        bias_ref[pl.ds(pl.multiple_of(page * PAGE, PAGE), PAGE), :] = bias
        return carry

    lax.fori_loop(0, GROUPS * PAGES_DEV, one_bias, 0, unroll=8)


def path_masks(first, table, left):
    return pl.pallas_call(
        mask_kernel,
        out_shape=(
            jax.ShapeDtypeStruct((GROUPS * PAGES_DEV, HD), jnp.int32),
            jax.ShapeDtypeStruct((GROUPS * PAGES_DEV * PAGE, HD), jnp.bfloat16),
        ),
        in_specs=[
            pl.BlockSpec(memory_space=pltpu.SMEM),
            pl.BlockSpec(memory_space=pltpu.VMEM),
            pl.BlockSpec(memory_space=pltpu.VMEM),
        ],
        out_specs=(pl.BlockSpec(memory_space=pltpu.VMEM), pl.BlockSpec(memory_space=pltpu.VMEM)),
        cost_estimate=pl.CostEstimate(flops=2**26, bytes_accessed=2**21, transcendentals=0),
        compiler_params=pltpu.CompilerParams(vmem_limit_bytes=16 * MIB),
        name="path_masks",
    )(first, table, left)


def attend_kernel(
    place_ref, tiles_ref, query_ref, a_ref, b_ref, c_ref, d_ref, bias_ref, out_ref,
    keys, values, rows, summed, top,
):
    for group, kv_ref in enumerate((a_ref, b_ref, c_ref, d_ref)):

        def one_page(page, carry, group=group, kv_ref=kv_ref):
            source = pl.ds(pl.multiple_of(page * PAGE, PAGE), PAGE)
            number = group * PAGES_DEV + page
            target = pl.ds(pl.multiple_of(place_ref[number] * PAGE, PAGE), PAGE)
            keys[target, 0:HD] = kv_ref[0, source, :]
            keys[target, HD : 2 * HD] = bias_ref[pl.ds(pl.multiple_of(number * PAGE, PAGE), PAGE), :]
            values[target, 0:HD] = kv_ref[1, source, :]
            return carry

        lax.fori_loop(0, PAGES_DEV, one_page, 0, unroll=8)
    values[:, HD : 2 * HD] = jnp.ones((values.shape[0], HD), jnp.bfloat16)
    for block in range(RING):
        held = query_ref[block]
        for head in range(HEADS):
            at = block * ROWS + head * CS
            rows[at : at + CS, 0:HD] = held[:, head * HD : (head + 1) * HD]
            rows[at : at + CS, HD : 2 * HD] = held[:, HEADS * HD : (HEADS + 1) * HD]
    summed[...] = jnp.zeros_like(summed)
    top[...] = jnp.full_like(top, LOW)

    def one_tile(tile, carry):
        here = pl.ds(pl.multiple_of(tile * TILE, TILE), TILE)
        for block in range(RING):
            span = slice(block * ROWS, (block + 1) * ROWS)
            scores = lax.dot_general(
                rows[span, :], keys[here, :], (((1,), (1,)), ((), ())),
                preferred_element_type=jnp.float32,
            )
            old = top[span, :]
            new = jnp.maximum(old, jnp.max(scores, axis=1, keepdims=True) * C2)
            weights = jnp.exp2(scores * C2 - new[:, 0:1]).astype(jnp.bfloat16)
            factor = jnp.exp2(old - new)
            part = jnp.dot(weights, values[here, :], preferred_element_type=jnp.float32)
            summed[span, 0:HD] = summed[span, 0:HD] * factor + part[:, 0:HD]
            summed[span, HD : 2 * HD] = summed[span, HD : 2 * HD] * factor + part[:, HD : 2 * HD]
            top[span, :] = new
        return carry

    lax.fori_loop(0, tiles_ref[0], one_tile, 0)
    diagonal = lax.broadcasted_iota(jnp.int32, (HD, HD), 0) == lax.broadcasted_iota(jnp.int32, (HD, HD), 1)
    for block in range(RING):
        span = slice(block * ROWS, (block + 1) * ROWS)
        total = summed[span, HD : 2 * HD]
        out_ref[block, 0:ROWS, :] = (summed[span, 0:HD] / total).astype(jnp.bfloat16)
        level = top[span, :] + jnp.log2(total)
        lines = [
            jnp.sum(jnp.where(diagonal, level[half * HD : (half + 1) * HD], 0.0), axis=0, keepdims=True)
            for half in range(2)
        ]
        line = jnp.concatenate(lines, axis=0)
        high = line.astype(jnp.bfloat16).astype(jnp.float32)
        middle = (line - high).astype(jnp.bfloat16).astype(jnp.float32)
        low = line - high - middle
        tail = jnp.concatenate([high, middle, low, jnp.zeros((10, HD), jnp.float32)], axis=0)
        out_ref[block, ROWS : ROWS + 16, :] = tail.astype(jnp.bfloat16)


def attend(place, tiles, query, kvs, bias):
    tokens = GROUPS * PAGES_DEV * PAGE
    vmem = pl.BlockSpec(memory_space=pltpu.VMEM)
    smem = pl.BlockSpec(memory_space=pltpu.SMEM)
    return pl.pallas_call(
        attend_kernel,
        out_shape=jax.ShapeDtypeStruct((RING, ROWS + 16, HD), jnp.bfloat16),
        in_specs=[smem, smem] + [vmem] * 6,
        out_specs=vmem,
        scratch_shapes=[
            pltpu.VMEM((tokens, 2 * HD), jnp.bfloat16),
            pltpu.VMEM((tokens, 2 * HD), jnp.bfloat16),
            pltpu.VMEM((RING * ROWS, 2 * HD), jnp.bfloat16),
            pltpu.VMEM((RING * ROWS, 2 * HD), jnp.float32),
            pltpu.VMEM((RING * ROWS, HD), jnp.float32),
        ],
        cost_estimate=pl.CostEstimate(flops=2**33, bytes_accessed=2**23, transcendentals=2**23),
        compiler_params=pltpu.CompilerParams(vmem_limit_bytes=48 * MIB),
        name="attend",
    )(place, tiles, query, *kvs, bias)


def finish_kernel(
    parts_ref, query_ref, key_ref, value_ref, allowed_ref, alive_ref, weight_ref, out_ref, attended
):
    @pl.when(pl.program_id(0) == 0)
    def merge():
        diagonal = lax.broadcasted_iota(jnp.int32, (HD, HD), 0) == lax.broadcasted_iota(jnp.int32, (HD, HD), 1)
        levels = []
        for block in range(RING):
            tail = parts_ref[block, ROWS : ROWS + 16, :].astype(jnp.float32)
            line = tail[0:2] + tail[2:4] + tail[4:6]
            columns = [
                jnp.sum(jnp.where(diagonal, jnp.broadcast_to(line[half : half + 1], (HD, HD)), 0.0), axis=1, keepdims=True)
                for half in range(2)
            ]
            levels.append(jnp.concatenate(columns, axis=0))
        query = jnp.concatenate([query_ref[:, head * HD : (head + 1) * HD] for head in range(HEADS)], axis=0)
        scores = lax.dot_general(
            query, key_ref[...], (((1,), (1,)), ((), ())), preferred_element_type=jnp.float32
        )
        allowed = jnp.concatenate([allowed_ref[...]] * HEADS, axis=0) > 0
        scores = jnp.where(allowed, scores * C2, -BIG)
        own_top = jnp.max(scores, axis=1, keepdims=True)
        own = jnp.where(allowed, jnp.exp2(scores - own_top), 0.0)
        own_sum = jnp.dot(own.astype(jnp.bfloat16), value_ref[...], preferred_element_type=jnp.float32)
        best = own_top
        for level in levels:
            best = jnp.maximum(best, level)
        factor = jnp.exp2(own_top - best)
        total = factor * jnp.sum(own, axis=1, keepdims=True)
        summed = factor * own_sum
        for block in range(RING):
            factor = jnp.exp2(levels[block] - best)
            total = total + factor
            summed = summed + factor * parts_ref[block, 0:ROWS, :].astype(jnp.float32)
        result = (summed / total).astype(jnp.bfloat16)
        for head in range(HEADS):
            attended[:, head * HD : (head + 1) * HD] = result[head * CS : (head + 1) * CS, :]

    terms = jnp.dot(attended[...], weight_ref[...], preferred_element_type=jnp.float32)
    out_ref[0] = (terms * alive_ref[...]).astype(jnp.bfloat16)


def finish(parts, query, keys, values, allowed, alive, weight):
    blocks = 8
    width = weight.shape[1] // blocks

    def whole(shape):
        return pl.BlockSpec(shape, lambda i: (0,) * len(shape))

    return pl.pallas_call(
        finish_kernel,
        grid=(blocks,),
        out_shape=jax.ShapeDtypeStruct((blocks, CS, width), jnp.bfloat16),
        in_specs=[
            whole(parts.shape),
            whole(query.shape),
            whole(keys.shape),
            whole(values.shape),
            whole(allowed.shape),
            whole(alive.shape),
            pl.BlockSpec((weight.shape[0], width), lambda i: (0, i)),
        ],
        out_specs=pl.BlockSpec((1, CS, width), lambda i: (i, 0, 0)),
        scratch_shapes=[pltpu.VMEM((CS, HEADS * HD), jnp.bfloat16)],
        cost_estimate=pl.CostEstimate(flops=2**28, bytes_accessed=2**23, transcendentals=0),
        compiler_params=pltpu.CompilerParams(vmem_limit_bytes=32 * MIB),
        name="finish",
    )(parts, query, keys, values, allowed, alive, weight)


def body(
    queries, new_keys, new_values, pool_keys, pool_values, out_weight, page_table, prefix_len, parent, finished
):
    children, steps, width = queries.shape
    rows = children * steps
    nodes, path_pages = page_table.shape
    query = queries.reshape(rows, width)
    node_of_row = jnp.repeat(parent, steps)
    hot = (node_of_row[:, None] == jnp.arange(HD, dtype=jnp.int32)[None, :]).astype(jnp.bfloat16)
    sent = jnp.concatenate([query, hot], axis=1)
    gathered = lax.all_to_all(
        jnp.broadcast_to(sent[None], (RING,) + sent.shape), "z", split_axis=0, concat_axis=0, tiled=True
    )

    swap = [(0, 1), (1, 0)]
    kv = jnp.stack([pool_keys.reshape(PAGES_DEV * PAGE, HD), pool_values.reshape(PAGES_DEV * PAGE, HD)])
    kv_far = lax.ppermute(kv, "yh", swap)
    kv_core = lax.ppermute(kv, "c", swap)
    kv_far_core = lax.ppermute(kv_far, "c", swap)
    yh, z, core = lax.axis_index("yh"), lax.axis_index("z"), lax.axis_index("c")
    first = jnp.stack(
        [
            PAGES_DEV * ((a * RING + z) * 2 + b)
            for a, b in ((yh, core), (yh, 1 - core), (1 - yh, core), (1 - yh, 1 - core))
        ]
    ).astype(jnp.int32)
    table = page_table.T.reshape(nodes * path_pages // HD, HD)
    place = jnp.arange(path_pages, dtype=jnp.int32)
    left = jnp.clip(prefix_len[None, :] - PAGE * place[:, None], 0, PAGE).reshape(table.shape)
    count, bias = path_masks(first, table, left)
    uses = jnp.sum((count[:, :nodes] > 0).astype(jnp.int32), axis=1)
    order = jnp.arange(uses.shape[0], dtype=jnp.int32)
    before = (uses[None, :] > uses[:, None]) | ((uses[None, :] == uses[:, None]) & (order[None, :] < order[:, None]))
    rank = jnp.sum(before.astype(jnp.int32), axis=1)
    used = jnp.sum((uses > 0).astype(jnp.int32))
    tiles = jnp.maximum((used * PAGE + TILE - 1) // TILE, 1).reshape(1)
    parts = attend(rank, tiles, gathered, (kv, kv_core, kv_far, kv_far_core), bias)
    parts = lax.all_to_all(parts, "z", split_axis=0, concat_axis=0, tiled=True)

    alive = 1 - finished
    child = jnp.arange(rows, dtype=jnp.int32) // steps
    step = jnp.arange(rows, dtype=jnp.int32) % steps
    allowed = (
        (child[:, None] == child[None, :])
        & (step[None, :] <= step[:, None])
        & (alive.reshape(1, rows) > 0)
    ).astype(jnp.int32)
    terms = finish(
        parts,
        query,
        new_keys.reshape(rows, HD),
        new_values.reshape(rows, HD),
        allowed,
        alive.reshape(rows, 1).astype(jnp.float32),
        out_weight,
    )
    terms = lax.all_to_all(terms, ("yl", "x"), split_axis=0, concat_axis=0, tiled=True)
    return jnp.sum(terms.astype(jnp.float32), axis=0).reshape(children, steps, terms.shape[-1])


def solution(mesh):
    fine = Mesh(mesh.devices.reshape(2, RING, 2, 2, 4), ("yh", "z", "c", "yl", "x"))
    branch, tensor = ("yh", "z", "c"), ("yl", "x")
    placed = (
        P(branch, None, tensor),
        P(branch, None, tensor),
        P(branch, None, tensor),
        P(branch, None, tensor),
        P(branch, None, tensor),
        P(tensor, None),
        P(),
        P(),
        P(branch),
        P(branch, None),
    )
    return jax.shard_map(
        body, mesh=fine, in_specs=placed, out_specs=P(branch, None, tensor), check_vma=False
    )
```

```python
import functools

import jax
import jax.numpy as jnp
from jax import lax
from jax.experimental import pallas as pl
from jax.experimental.pallas import tpu as pltpu
from jax.sharding import Mesh, PartitionSpec as P

HD = 128
PAGE = 16
PAGES_DEV = 96
GROUPS = 4
RING = 8
ROWS = 256
HEADS = 8
CS = 32
UNROLL = 8
TOGETHER = 2
SIZES = (2304, 2560, 6144)
BIG = 2.0**100
C2 = HD**-0.5 * 1.4426950408889634
MIB = 1024 * 1024


def cost(microseconds):
    return pl.CostEstimate(flops=int(microseconds * 1.15e9), bytes_accessed=2**16, transcendentals=0)


def prepare_kernel(parent_ref, query_ref, out_ref, wide):
    lane = lax.broadcasted_iota(jnp.int32, (4, HD), 1)
    for child in range(8):
        rows = slice(child * 4, child * 4 + 4)
        wide[rows, 0 : HEADS * HD] = query_ref[child].astype(jnp.float32)
        wide[rows, HEADS * HD : (HEADS + 1) * HD] = jnp.where(lane == parent_ref[child], 1.0, 0.0)
    held = wide[...].astype(jnp.bfloat16)
    for copy in range(RING):
        out_ref[copy] = held


def prepare(parent, queries):
    return pl.pallas_call(
        prepare_kernel,
        out_shape=jax.ShapeDtypeStruct((RING, CS, (HEADS + 1) * HD), jnp.bfloat16),
        in_specs=[pl.BlockSpec(memory_space=pltpu.SMEM), pl.BlockSpec(memory_space=pltpu.VMEM)],
        out_specs=pl.BlockSpec(memory_space=pltpu.VMEM),
        scratch_shapes=[pltpu.VMEM((CS, (HEADS + 1) * HD), jnp.float32)],
        cost_estimate=cost(1.0),
        compiler_params=pltpu.CompilerParams(vmem_limit_bytes=60 * MIB),
        name="prepare",
    )(parent, queries)


def mask_kernel(first_ref, table_ref, left_ref, count_ref):
    left = left_ref[...]
    for block in range(GROUPS):
        first = first_ref[block]

        def one_page(page, carry, block=block, first=first):
            hit = jnp.where(table_ref[...] == first + page, left, 0)
            count_ref[pl.ds(block * PAGES_DEV + page, 1), :] = jnp.sum(hit, axis=0, keepdims=True)
            return carry

        lax.fori_loop(0, PAGES_DEV, one_page, 0, unroll=8)
    part = count_ref[...]
    part = part + pltpu.roll(part, 64, 1)
    count_ref[...] = part + pltpu.roll(part, 32, 1)


def path_masks(first, table, left):
    return pl.pallas_call(
        mask_kernel,
        out_shape=jax.ShapeDtypeStruct((GROUPS * PAGES_DEV, HD), jnp.int32),
        in_specs=[
            pl.BlockSpec(memory_space=pltpu.SMEM),
            pl.BlockSpec(memory_space=pltpu.VMEM),
            pl.BlockSpec(memory_space=pltpu.VMEM),
        ],
        out_specs=pl.BlockSpec(memory_space=pltpu.VMEM),
        cost_estimate=cost(7.0),
        compiler_params=pltpu.CompilerParams(vmem_limit_bytes=16 * MIB),
        name="path_masks",
    )(first, table, left)


def attend_tokens(tokens, rows, keys, values, levels, out_ref):
    def span(block):
        return pl.ds(pl.multiple_of(block * ROWS, ROWS), ROWS)

    def score(block):
        return lax.dot_general(
            rows[span(block), :], keys[0:tokens, :], (((1,), (1,)), ((), ())),
            preferred_element_type=jnp.float32,
        )

    def weigh(scores):
        top = jnp.max(scores, axis=1, keepdims=True) * C2
        return top, jnp.exp2(scores * C2 - top).astype(jnp.bfloat16)

    def store(block, top, weights):
        summed = jnp.dot(weights, values[0:tokens, :], preferred_element_type=jnp.float32)
        total = summed[:, HD : 2 * HD]
        out_ref[block, 0:ROWS, :] = (summed[:, 0:HD] / total).astype(jnp.bfloat16)
        levels[span(block), :] = top + jnp.log2(total)

    def some_blocks(step, carry):
        first = step * TOGETHER
        scores, held = score(first), None
        for index in range(TOGETHER):
            following = score(first + index + 1) if index + 1 < TOGETHER else None
            top, weights = weigh(scores)
            if held is not None:
                store(*held)
            held, scores = (first + index, top, weights), following
        store(*held)
        return carry

    lax.fori_loop(0, RING // TOGETHER, some_blocks, 0)


def attend_kernel(
    list_ref, used_ref, query_ref, ka_ref, va_ref, kb_ref, vb_ref, kc_ref, vc_ref, kd_ref, vd_ref,
    count_ref, out_ref, keys, values, rows, levels,
):
    token = lax.broadcasted_iota(jnp.int32, (PAGE, HD), 0)
    pool = ((ka_ref, va_ref), (kb_ref, vb_ref), (kc_ref, vc_ref), (kd_ref, vd_ref))
    filled = jnp.int32(0)
    for group, (key_ref, value_ref) in enumerate(pool):

        def some_pages(step, carry, group=group, key_ref=key_ref, value_ref=value_ref, filled=filled):
            for lane in range(UNROLL):
                page = list_ref[group * PAGES_DEV + step * UNROLL + lane]
                target = pl.ds(pl.multiple_of((filled + step * UNROLL + lane) * PAGE, PAGE), PAGE)
                keys[target, 0:HD] = key_ref[page]
                held = jnp.broadcast_to(count_ref[pl.ds(group * PAGES_DEV + page, 1), :], (PAGE, HD))
                keys[target, HD : 2 * HD] = jnp.where(token >= held, -BIG, 0.0).astype(jnp.bfloat16)
                values[target, 0:HD] = value_ref[page]
            return carry

        lax.fori_loop(0, (used_ref[group] + UNROLL - 1) // UNROLL, some_pages, 0)
        filled = filled + used_ref[group]
    values[:, HD : 2 * HD] = jnp.ones((values.shape[0], HD), jnp.bfloat16)
    for block in range(RING):
        held = query_ref[block]
        for head in range(HEADS):
            at = block * ROWS + head * CS
            rows[at : at + CS, 0:HD] = held[:, head * HD : (head + 1) * HD]
            rows[at : at + CS, HD : 2 * HD] = held[:, HEADS * HD : (HEADS + 1) * HD]

    lower = -1
    for tokens in SIZES:

        @pl.when((filled * PAGE > lower) & (filled * PAGE <= tokens))
        def run(tokens=tokens):
            def one_blank(page, carry):
                target = pl.ds(pl.multiple_of(page * PAGE, PAGE), PAGE)
                keys[target, 0:HD] = jnp.zeros((PAGE, HD), jnp.bfloat16)
                keys[target, HD : 2 * HD] = jnp.full((PAGE, HD), -BIG, jnp.bfloat16)
                values[target, 0:HD] = jnp.zeros((PAGE, HD), jnp.bfloat16)
                return carry

            lax.fori_loop(filled, tokens // PAGE, one_blank, 0)
            attend_tokens(tokens, rows, keys, values, levels, out_ref)

        lower = tokens
    diagonal = lax.broadcasted_iota(jnp.int32, (HD, HD), 0) == lax.broadcasted_iota(jnp.int32, (HD, HD), 1)
    for block in range(RING):
        level = levels[block * ROWS : (block + 1) * ROWS, :]
        lines = [
            jnp.sum(jnp.where(diagonal, level[half * HD : (half + 1) * HD], 0.0), axis=0, keepdims=True)
            for half in range(2)
        ]
        line = jnp.concatenate(lines, axis=0)
        high = line.astype(jnp.bfloat16).astype(jnp.float32)
        middle = (line - high).astype(jnp.bfloat16).astype(jnp.float32)
        low = line - high - middle
        tail = jnp.concatenate([high, middle, low, jnp.zeros((10, HD), jnp.float32)], axis=0)
        out_ref[block, ROWS : ROWS + 16, :] = tail.astype(jnp.bfloat16)


def attend(pages, used, query, pool, count):
    tokens = (GROUPS * PAGES_DEV + UNROLL) * PAGE
    vmem = pl.BlockSpec(memory_space=pltpu.VMEM)
    smem = pl.BlockSpec(memory_space=pltpu.SMEM)
    return pl.pallas_call(
        attend_kernel,
        out_shape=jax.ShapeDtypeStruct((RING, ROWS + 16, HD), jnp.bfloat16),
        in_specs=[smem, smem] + [vmem] * 10,
        out_specs=vmem,
        scratch_shapes=[
            pltpu.VMEM((tokens, 2 * HD), jnp.bfloat16),
            pltpu.VMEM((tokens, 2 * HD), jnp.bfloat16),
            pltpu.VMEM((RING * ROWS, 2 * HD), jnp.bfloat16),
            pltpu.VMEM((RING * ROWS, HD), jnp.float32),
        ],
        cost_estimate=cost(10.0),
        compiler_params=pltpu.CompilerParams(vmem_limit_bytes=40 * MIB),
        name="attend",
    )(pages, used, query, *pool, count)


def finish_kernel(
    parts_ref, query_ref, key_ref, value_ref, allowed_ref, alive_ref, weight_ref, out_ref, weights, ready
):
    width = out_ref.shape[2]
    copies = [
        pltpu.make_async_copy(
            weight_ref.at[:, part * width : (part + 1) * width], weights.at[part], ready.at[part]
        )
        for part in range(out_ref.shape[0])
    ]
    for copy in copies:
        copy.start()
    diagonal = lax.broadcasted_iota(jnp.int32, (HD, HD), 0) == lax.broadcasted_iota(jnp.int32, (HD, HD), 1)
    levels = []
    for block in range(RING):
        tail = parts_ref[block, ROWS : ROWS + 16, :].astype(jnp.float32)
        line = tail[0:2] + tail[2:4] + tail[4:6]
        columns = [
            jnp.sum(jnp.where(diagonal, jnp.broadcast_to(line[half : half + 1], (HD, HD)), 0.0), axis=1, keepdims=True)
            for half in range(2)
        ]
        levels.append(jnp.concatenate(columns, axis=0))
    query = jnp.concatenate([query_ref[0, :, head * HD : (head + 1) * HD] for head in range(HEADS)], axis=0)
    scores = lax.dot_general(
        query, key_ref[...], (((1,), (1,)), ((), ())), preferred_element_type=jnp.float32
    )
    allowed = jnp.concatenate([allowed_ref[...]] * HEADS, axis=0) > 0
    scores = jnp.where(allowed, scores * C2, -BIG)
    own_top = jnp.max(scores, axis=1, keepdims=True)
    own = jnp.where(allowed, jnp.exp2(scores - own_top), 0.0)
    own_sum = jnp.dot(own.astype(jnp.bfloat16), value_ref[...], preferred_element_type=jnp.float32)
    best = own_top
    for level in levels:
        best = jnp.maximum(best, level)
    factor = jnp.exp2(own_top - best)
    total = factor * jnp.sum(own, axis=1, keepdims=True)
    summed = factor * own_sum
    for block in range(RING):
        factor = jnp.exp2(levels[block] - best)
        total = total + factor
        summed = summed + factor * parts_ref[block, 0:ROWS, :].astype(jnp.float32)
    result = (summed / total).astype(jnp.bfloat16)
    attended = jnp.concatenate([result[head * CS : (head + 1) * CS, :] for head in range(HEADS)], axis=1)

    for part, copy in enumerate(copies):
        copy.wait()
        terms = jnp.dot(attended, weights[part], preferred_element_type=jnp.float32)
        out_ref[part] = (terms * alive_ref[...]).astype(jnp.bfloat16)


def finish(parts, query, keys, values, allowed, alive, weight):
    blocks = 8
    width = weight.shape[1] // blocks
    vmem = pl.BlockSpec(memory_space=pltpu.VMEM)
    return pl.pallas_call(
        finish_kernel,
        out_shape=jax.ShapeDtypeStruct((blocks, CS, width), jnp.bfloat16),
        in_specs=[vmem] * 6 + [pl.BlockSpec(memory_space=pltpu.HBM)],
        out_specs=vmem,
        scratch_shapes=[
            pltpu.VMEM((blocks, weight.shape[0], width), jnp.bfloat16),
            pltpu.SemaphoreType.DMA((blocks,)),
        ],
        cost_estimate=cost(4.0),
        compiler_params=pltpu.CompilerParams(vmem_limit_bytes=57 * MIB),
        name="finish",
    )(parts, query, keys, values, allowed, alive, weight)


def body(
    queries, new_keys, new_values, pool_keys, pool_values, out_weight, page_table, prefix_len, parent, finished
):
    children, steps, width = queries.shape
    rows = children * steps
    nodes, path_pages = page_table.shape
    sent = prepare(parent, queries)
    gathered = lax.all_to_all(sent, "z", split_axis=0, concat_axis=0, tiled=True)

    pool_values, sent = lax.optimization_barrier((pool_values, sent))

    def swap(values, axis):
        return [lax.ppermute(value, axis, [(0, 1), (1, 0)]) for value in values]

    kv = [pool_keys, pool_values]
    kv_far = swap(kv, "yh")
    kv_core = swap(kv, "c")
    yh, z, core = lax.axis_index("yh"), lax.axis_index("z"), lax.axis_index("c")
    first = jnp.stack(
        [
            PAGES_DEV * ((a * RING + z) * 2 + b)
            for a, b in ((yh, core), (yh, 1 - core), (1 - yh, core), (1 - yh, 1 - core))
        ]
    ).astype(jnp.int32)
    table = page_table.T.reshape(nodes * path_pages // HD, HD)
    place = jnp.arange(path_pages, dtype=jnp.int32)
    left = jnp.clip(prefix_len[None, :] - PAGE * place[:, None], 0, PAGE).reshape(table.shape)
    count = path_masks(first, table, left)
    kv_far[0], kv_far[1], count = lax.optimization_barrier((kv_far[0], kv_far[1], count))
    kv_far_core = swap(kv_far, "c")
    taken = jnp.any(count[:, :nodes] > 0, axis=1).reshape(GROUPS, PAGES_DEV)
    order = jnp.arange(PAGES_DEV, dtype=jnp.int32)
    earlier = taken[:, None, :] & (order[None, None, :] < order[None, :, None])
    rank = jnp.sum(earlier.astype(jnp.int32), axis=2)
    chosen = taken[:, :, None] & (rank[:, :, None] == order[None, None, :])
    pages = jnp.sum(jnp.where(chosen, order[None, :, None], 0), axis=1).reshape(GROUPS * PAGES_DEV)
    used = jnp.sum(taken.astype(jnp.int32), axis=1)
    parts = attend(pages, used, gathered, kv + kv_core + kv_far + kv_far_core, count)
    parts = lax.all_to_all(parts, "z", split_axis=0, concat_axis=0, tiled=True)

    alive = 1 - finished
    child = jnp.arange(rows, dtype=jnp.int32) // steps
    step = jnp.arange(rows, dtype=jnp.int32) % steps
    allowed = (
        (child[:, None] == child[None, :])
        & (step[None, :] <= step[:, None])
        & (alive.reshape(1, rows) > 0)
    ).astype(jnp.int32)
    terms = finish(
        parts,
        sent,
        new_keys.reshape(rows, HD),
        new_values.reshape(rows, HD),
        allowed,
        alive.reshape(rows, 1).astype(jnp.float32),
        out_weight,
    )
    terms = lax.all_to_all(terms, ("yl", "x"), split_axis=0, concat_axis=0, tiled=True)
    return jnp.sum(terms.astype(jnp.float32), axis=0).reshape(children, steps, terms.shape[-1])


def solution(mesh):
    fine = Mesh(mesh.devices.reshape(2, RING, 2, 2, 4), ("yh", "z", "c", "yl", "x"))
    branch, tensor = ("yh", "z", "c"), ("yl", "x")
    placed = (
        P(branch, None, tensor),
        P(branch, None, tensor),
        P(branch, None, tensor),
        P(branch, None, tensor),
        P(branch, None, tensor),
        P(tensor, None),
        P(),
        P(),
        P(branch),
        P(branch, None),
    )
    return jax.shard_map(
        body, mesh=fine, in_specs=placed, out_specs=P(branch, None, tensor), check_vma=False
    )
```

```python
import functools

import jax
import jax.numpy as jnp
from jax import lax
from jax.experimental import pallas as pl
from jax.experimental.pallas import tpu as pltpu
from jax.sharding import Mesh, PartitionSpec as P

HD = 128
PAGE = 16
PAGES_DEV = 96
GROUPS = 4
RING = 8
ROWS = 256
HEADS = 8
CS = 32
UNROLL = 8
TOGETHER = 2
SIZES = (2304, 2560, 6144)
BIG = 2.0**100
C2 = HD**-0.5 * 1.4426950408889634
MIB = 1024 * 1024


def cost(microseconds):
    return pl.CostEstimate(flops=int(microseconds * 1.15e9), bytes_accessed=2**16, transcendentals=0)


def prepare_kernel(parent_ref, query_ref, out_ref, wide):
    lane = lax.broadcasted_iota(jnp.int32, (4, HD), 1)
    for child in range(8):
        rows = slice(child * 4, child * 4 + 4)
        wide[rows, 0 : HEADS * HD] = query_ref[child].astype(jnp.float32)
        wide[rows, HEADS * HD : (HEADS + 1) * HD] = jnp.where(lane == parent_ref[child], 1.0, 0.0)
    held = wide[...].astype(jnp.bfloat16)
    for copy in range(RING):
        out_ref[copy] = held


def prepare(parent, queries):
    return pl.pallas_call(
        prepare_kernel,
        out_shape=jax.ShapeDtypeStruct((RING, CS, (HEADS + 1) * HD), jnp.bfloat16),
        in_specs=[pl.BlockSpec(memory_space=pltpu.SMEM), pl.BlockSpec(memory_space=pltpu.VMEM)],
        out_specs=pl.BlockSpec(memory_space=pltpu.VMEM),
        scratch_shapes=[pltpu.VMEM((CS, (HEADS + 1) * HD), jnp.float32)],
        cost_estimate=cost(1.0),
        compiler_params=pltpu.CompilerParams(vmem_limit_bytes=60 * MIB),
        name="prepare",
    )(parent, queries)


def mask_kernel(first_ref, table_ref, left_ref, count_ref):
    left = left_ref[...]
    for block in range(GROUPS):
        first = first_ref[block]

        def one_page(page, carry, block=block, first=first):
            hit = jnp.where(table_ref[...] == first + page, left, 0)
            count_ref[pl.ds(block * PAGES_DEV + page, 1), :] = jnp.sum(hit, axis=0, keepdims=True)
            return carry

        lax.fori_loop(0, PAGES_DEV, one_page, 0, unroll=8)
    part = count_ref[...]
    part = part + pltpu.roll(part, 64, 1)
    count_ref[...] = part + pltpu.roll(part, 32, 1)


def path_masks(first, table, left):
    return pl.pallas_call(
        mask_kernel,
        out_shape=jax.ShapeDtypeStruct((GROUPS * PAGES_DEV, HD), jnp.int32),
        in_specs=[
            pl.BlockSpec(memory_space=pltpu.SMEM),
            pl.BlockSpec(memory_space=pltpu.VMEM),
            pl.BlockSpec(memory_space=pltpu.VMEM),
        ],
        out_specs=pl.BlockSpec(memory_space=pltpu.VMEM),
        cost_estimate=cost(7.0),
        compiler_params=pltpu.CompilerParams(vmem_limit_bytes=16 * MIB),
        name="path_masks",
    )(first, table, left)


def attend_tokens(tokens, rows, keys, values, levels, out_ref):
    chunk = 2 * ROWS if tokens < 3000 else ROWS

    def span(block):
        return pl.ds(pl.multiple_of(block * chunk, chunk), chunk)

    def score(block):
        return lax.dot_general(
            rows[span(block), :], keys[0:tokens, :], (((1,), (1,)), ((), ())),
            preferred_element_type=jnp.float32,
        )

    def weigh(scores):
        top = jnp.max(scores, axis=1, keepdims=True) * C2
        return top, jnp.exp2(scores * C2 - top).astype(jnp.bfloat16)

    def store(block, top, weights):
        summed = jnp.dot(weights, values[0:tokens, :], preferred_element_type=jnp.float32)
        total = summed[:, HD : 2 * HD]
        result = (summed[:, 0:HD] / total).astype(jnp.bfloat16)
        for part in range(chunk // ROWS):
            out_ref[block * (chunk // ROWS) + part, 0:ROWS, :] = result[part * ROWS : (part + 1) * ROWS]
        levels[span(block), :] = top + jnp.log2(total)

    def some_blocks(step, carry):
        first = step * TOGETHER
        scores, held = score(first), None
        for index in range(TOGETHER):
            following = score(first + index + 1) if index + 1 < TOGETHER else None
            top, weights = weigh(scores)
            if held is not None:
                store(*held)
            held, scores = (first + index, top, weights), following
        store(*held)
        return carry

    lax.fori_loop(0, RING * ROWS // chunk // TOGETHER, some_blocks, 0)


def attend_kernel(
    list_ref, used_ref, query_ref, ka_ref, va_ref, kb_ref, vb_ref, kc_ref, vc_ref, kd_ref, vd_ref,
    count_ref, out_ref, keys, values, rows, levels,
):
    token = lax.broadcasted_iota(jnp.int32, (PAGE, HD), 0)
    pool = ((ka_ref, va_ref), (kb_ref, vb_ref), (kc_ref, vc_ref), (kd_ref, vd_ref))
    filled = jnp.int32(0)
    for group, (key_ref, value_ref) in enumerate(pool):

        def some_pages(step, carry, group=group, key_ref=key_ref, value_ref=value_ref, filled=filled):
            for lane in range(UNROLL):
                page = list_ref[group * PAGES_DEV + step * UNROLL + lane]
                target = pl.ds(pl.multiple_of((filled + step * UNROLL + lane) * PAGE, PAGE), PAGE)
                keys[target, 0:HD] = key_ref[page]
                held = jnp.broadcast_to(count_ref[pl.ds(group * PAGES_DEV + page, 1), :], (PAGE, HD))
                keys[target, HD : 2 * HD] = jnp.where(token >= held, -BIG, 0.0).astype(jnp.bfloat16)
                values[target, 0:HD] = value_ref[page]
            return carry

        lax.fori_loop(0, (used_ref[group] + UNROLL - 1) // UNROLL, some_pages, 0)
        filled = filled + used_ref[group]
    values[:, HD : 2 * HD] = jnp.ones((values.shape[0], HD), jnp.bfloat16)
    for block in range(RING):
        held = query_ref[block]
        for head in range(HEADS):
            at = block * ROWS + head * CS
            rows[at : at + CS, 0:HD] = held[:, head * HD : (head + 1) * HD]
            rows[at : at + CS, HD : 2 * HD] = held[:, HEADS * HD : (HEADS + 1) * HD]

    lower = -1
    for tokens in SIZES:

        @pl.when((filled * PAGE > lower) & (filled * PAGE <= tokens))
        def run(tokens=tokens):
            def one_blank(page, carry):
                target = pl.ds(pl.multiple_of(page * PAGE, PAGE), PAGE)
                keys[target, 0:HD] = jnp.zeros((PAGE, HD), jnp.bfloat16)
                keys[target, HD : 2 * HD] = jnp.full((PAGE, HD), -BIG, jnp.bfloat16)
                values[target, 0:HD] = jnp.zeros((PAGE, HD), jnp.bfloat16)
                return carry

            lax.fori_loop(filled, tokens // PAGE, one_blank, 0)
            attend_tokens(tokens, rows, keys, values, levels, out_ref)

        lower = tokens
    diagonal = lax.broadcasted_iota(jnp.int32, (HD, HD), 0) == lax.broadcasted_iota(jnp.int32, (HD, HD), 1)
    for block in range(RING):
        level = levels[block * ROWS : (block + 1) * ROWS, :]
        lines = [
            jnp.sum(jnp.where(diagonal, level[half * HD : (half + 1) * HD], 0.0), axis=0, keepdims=True)
            for half in range(2)
        ]
        line = jnp.concatenate(lines, axis=0)
        high = line.astype(jnp.bfloat16).astype(jnp.float32)
        middle = (line - high).astype(jnp.bfloat16).astype(jnp.float32)
        low = line - high - middle
        tail = jnp.concatenate([high, middle, low, jnp.zeros((10, HD), jnp.float32)], axis=0)
        out_ref[block, ROWS : ROWS + 16, :] = tail.astype(jnp.bfloat16)


def attend(pages, used, query, pool, count):
    tokens = (GROUPS * PAGES_DEV + UNROLL) * PAGE
    vmem = pl.BlockSpec(memory_space=pltpu.VMEM)
    smem = pl.BlockSpec(memory_space=pltpu.SMEM)
    return pl.pallas_call(
        attend_kernel,
        out_shape=jax.ShapeDtypeStruct((RING, ROWS + 16, HD), jnp.bfloat16),
        in_specs=[smem, smem] + [vmem] * 10,
        out_specs=vmem,
        scratch_shapes=[
            pltpu.VMEM((tokens, 2 * HD), jnp.bfloat16),
            pltpu.VMEM((tokens, 2 * HD), jnp.bfloat16),
            pltpu.VMEM((RING * ROWS, 2 * HD), jnp.bfloat16),
            pltpu.VMEM((RING * ROWS, HD), jnp.float32),
        ],
        cost_estimate=cost(10.0),
        compiler_params=pltpu.CompilerParams(vmem_limit_bytes=30 * MIB),
        name="attend",
    )(pages, used, query, *pool, count)


def permit_kernel(finished_ref, allowed_ref, alive_ref):
    row = lax.broadcasted_iota(jnp.int32, (CS, HD), 0)
    column = lax.broadcasted_iota(jnp.int32, (CS, HD), 1)
    same = (row // 4 == column // 4) & (column <= row)
    alive = 1 - finished_ref[...]
    allowed_ref[...] = jnp.where(same, jnp.broadcast_to(alive, (CS, HD)), 0)
    own = jnp.where(row == column, jnp.broadcast_to(alive, (CS, HD)), 0)
    alive_ref[...] = jnp.broadcast_to(jnp.sum(own, axis=1, keepdims=True), (CS, HD)).astype(jnp.float32)


def permit(finished):
    vmem = pl.BlockSpec(memory_space=pltpu.VMEM)
    return pl.pallas_call(
        permit_kernel,
        out_shape=(jax.ShapeDtypeStruct((CS, HD), jnp.int32), jax.ShapeDtypeStruct((CS, HD), jnp.float32)),
        in_specs=[vmem],
        out_specs=(vmem, vmem),
        cost_estimate=cost(15.0),
        compiler_params=pltpu.CompilerParams(vmem_limit_bytes=2 * MIB),
        name="permit",
    )(finished)


def finish_kernel(
    parts_ref, query_ref, key_ref, value_ref, allowed_ref, alive_ref, weight_ref, out_ref
):
    width = out_ref.shape[2]
    diagonal = lax.broadcasted_iota(jnp.int32, (HD, HD), 0) == lax.broadcasted_iota(jnp.int32, (HD, HD), 1)
    levels = []
    for block in range(RING):
        tail = parts_ref[block, ROWS : ROWS + 16, :].astype(jnp.float32)
        line = tail[0:2] + tail[2:4] + tail[4:6]
        columns = [
            jnp.sum(jnp.where(diagonal, jnp.broadcast_to(line[half : half + 1], (HD, HD)), 0.0), axis=1, keepdims=True)
            for half in range(2)
        ]
        levels.append(jnp.concatenate(columns, axis=0))
    query = jnp.concatenate([query_ref[0, :, head * HD : (head + 1) * HD] for head in range(HEADS)], axis=0)
    scores = lax.dot_general(
        query, key_ref[...], (((1,), (1,)), ((), ())), preferred_element_type=jnp.float32
    )
    allowed = jnp.concatenate([allowed_ref[:, 0:CS]] * HEADS, axis=0) > 0
    scores = jnp.where(allowed, scores * C2, -BIG)
    own_top = jnp.max(scores, axis=1, keepdims=True)
    own = jnp.where(allowed, jnp.exp2(scores - own_top), 0.0)
    own_sum = jnp.dot(own.astype(jnp.bfloat16), value_ref[...], preferred_element_type=jnp.float32)
    best = own_top
    for level in levels:
        best = jnp.maximum(best, level)
    factor = jnp.exp2(own_top - best)
    total = factor * jnp.sum(own, axis=1, keepdims=True)
    summed = factor * own_sum
    for block in range(RING):
        factor = jnp.exp2(levels[block] - best)
        total = total + factor
        summed = summed + factor * parts_ref[block, 0:ROWS, :].astype(jnp.float32)
    result = (summed / total).astype(jnp.bfloat16)
    attended = jnp.concatenate([result[head * CS : (head + 1) * CS, :] for head in range(HEADS)], axis=1)

    for part in range(out_ref.shape[0]):
        columns = weight_ref[:, part * width : (part + 1) * width]
        terms = jnp.dot(attended, columns, preferred_element_type=jnp.float32)
        out_ref[part] = (terms * alive_ref[:, 0:1]).astype(jnp.bfloat16)


def finish(parts, query, keys, values, allowed, alive, weight):
    blocks = 8
    width = weight.shape[1] // blocks
    vmem = pl.BlockSpec(memory_space=pltpu.VMEM)
    return pl.pallas_call(
        finish_kernel,
        out_shape=jax.ShapeDtypeStruct((blocks, CS, width), jnp.bfloat16),
        in_specs=[vmem] * 7,
        out_specs=vmem,
        cost_estimate=cost(4.0),
        compiler_params=pltpu.CompilerParams(vmem_limit_bytes=12 * MIB),
        name="finish",
    )(parts, query, keys, values, allowed, alive, weight)


def body(
    queries, new_keys, new_values, pool_keys, pool_values, out_weight, page_table, prefix_len, parent, finished
):
    children, steps, width = queries.shape
    rows = children * steps
    nodes, path_pages = page_table.shape
    sent = prepare(parent, queries)
    gathered = lax.all_to_all(sent, "z", split_axis=0, concat_axis=0, tiled=True)

    def swap(values, axis):
        return [lax.ppermute(value, axis, [(0, 1), (1, 0)]) for value in values]

    kv = [pool_keys, pool_values]
    kv_far = swap(kv, "yh")
    near_keys, near_values, sent = lax.optimization_barrier((pool_keys, pool_values, sent))
    kv_core = swap([near_keys, near_values], "c")
    yh, z, core = lax.axis_index("yh"), lax.axis_index("z"), lax.axis_index("c")
    first = jnp.stack(
        [
            PAGES_DEV * ((a * RING + z) * 2 + b)
            for a, b in ((yh, core), (yh, 1 - core), (1 - yh, core), (1 - yh, 1 - core))
        ]
    ).astype(jnp.int32)
    table = page_table.T.reshape(nodes * path_pages // HD, HD)
    place = jnp.arange(path_pages, dtype=jnp.int32)
    left = jnp.clip(prefix_len[None, :] - PAGE * place[:, None], 0, PAGE).reshape(table.shape)
    count = path_masks(first, table, left)
    kv_far[0], kv_far[1], count = lax.optimization_barrier((kv_far[0], kv_far[1], count))
    kv_far_core = swap(kv_far, "c")
    taken = jnp.any(count[:, :nodes] > 0, axis=1).reshape(GROUPS, PAGES_DEV)
    order = jnp.arange(PAGES_DEV, dtype=jnp.int32)
    earlier = taken[:, None, :] & (order[None, None, :] < order[None, :, None])
    rank = jnp.sum(earlier.astype(jnp.int32), axis=2)
    chosen = taken[:, :, None] & (rank[:, :, None] == order[None, None, :])
    pages = jnp.sum(jnp.where(chosen, order[None, :, None], 0), axis=1).reshape(GROUPS * PAGES_DEV)
    used = jnp.sum(taken.astype(jnp.int32), axis=1)
    parts = attend(pages, used, gathered, kv + kv_core + kv_far + kv_far_core, count)
    line = jnp.pad(finished.reshape(1, rows), ((0, 0), (0, HD - rows)), constant_values=1)
    parts, line = lax.optimization_barrier((parts, line))
    allowed, alive = permit(line)
    parts = lax.all_to_all(parts, "z", split_axis=0, concat_axis=0, tiled=True)

    terms = finish(
        parts,
        sent,
        new_keys.reshape(rows, HD),
        new_values.reshape(rows, HD),
        allowed,
        alive,
        out_weight,
    )
    terms = lax.all_to_all(terms, ("yl", "x"), split_axis=0, concat_axis=0, tiled=True)
    return jnp.sum(terms.astype(jnp.float32), axis=0).reshape(children, steps, terms.shape[-1])


def solution(mesh):
    fine = Mesh(mesh.devices.reshape(2, RING, 2, 2, 4), ("yh", "z", "c", "yl", "x"))
    branch, tensor = ("yh", "z", "c"), ("yl", "x")
    placed = (
        P(branch, None, tensor),
        P(branch, None, tensor),
        P(branch, None, tensor),
        P(branch, None, tensor),
        P(branch, None, tensor),
        P(tensor, None),
        P(),
        P(),
        P(branch),
        P(branch, None),
    )
    return jax.shard_map(
        body, mesh=fine, in_specs=placed, out_specs=P(branch, None, tensor), check_vma=False
    )
```

```python
import functools

import jax
import jax.numpy as jnp
from jax import lax
from jax.experimental import pallas as pl
from jax.experimental.pallas import tpu as pltpu
from jax.sharding import Mesh, PartitionSpec as P

HD = 128
PAGE = 16
PAGES_DEV = 96
GROUPS = 4
RING = 8
ROWS = 256
HEADS = 8
CS = 32
UNROLL = 8
TOGETHER = 2
SIZES = (2304, 2560, 6144)
BIG = 2.0**100
C2 = HD**-0.5 * 1.4426950408889634
MIB = 1024 * 1024


def cost(microseconds):
    return pl.CostEstimate(flops=int(microseconds * 1.15e9), bytes_accessed=2**16, transcendentals=0)


def prepare_kernel(parent_ref, query_ref, out_ref, wide):
    child = lax.broadcasted_iota(jnp.int32, (16, HD), 0)
    lane = lax.broadcasted_iota(jnp.int32, (16, HD), 1)
    hot = jnp.zeros((16, HD), jnp.float32)
    for number in range(8):
        wide[number * 4 : number * 4 + 4, :] = query_ref[number].astype(jnp.float32)
        hot = jnp.where((child == number) & (lane == parent_ref[number]), 1.0, hot)
    hot = hot.astype(jnp.bfloat16)
    held = wide[...].astype(jnp.bfloat16)
    for copy in range(RING):
        for head in range(HEADS):
            out_ref[copy, head * CS : (head + 1) * CS, :] = held[:, head * HD : (head + 1) * HD]
        out_ref[copy, ROWS : ROWS + 16, :] = hot


def prepare(parent, queries):
    return pl.pallas_call(
        prepare_kernel,
        out_shape=jax.ShapeDtypeStruct((RING, ROWS + 16, HD), jnp.bfloat16),
        in_specs=[pl.BlockSpec(memory_space=pltpu.SMEM), pl.BlockSpec(memory_space=pltpu.VMEM)],
        out_specs=pl.BlockSpec(memory_space=pltpu.VMEM),
        scratch_shapes=[pltpu.VMEM((CS, HEADS * HD), jnp.float32)],
        cost_estimate=cost(1.0),
        compiler_params=pltpu.CompilerParams(vmem_limit_bytes=60 * MIB),
        name="prepare",
    )(parent, queries)


def mask_kernel(first_ref, table_ref, left_ref, count_ref):
    left = left_ref[...]
    for block in range(GROUPS):
        first = first_ref[block]

        def one_page(page, carry, block=block, first=first):
            hit = jnp.where(table_ref[...] == first + page, left, 0)
            count_ref[pl.ds(block * PAGES_DEV + page, 1), :] = jnp.sum(hit, axis=0, keepdims=True)
            return carry

        lax.fori_loop(0, PAGES_DEV, one_page, 0, unroll=8)
    part = count_ref[...]
    part = part + pltpu.roll(part, 64, 1)
    count_ref[...] = part + pltpu.roll(part, 32, 1)


def path_masks(first, table, left):
    return pl.pallas_call(
        mask_kernel,
        out_shape=jax.ShapeDtypeStruct((GROUPS * PAGES_DEV, HD), jnp.int32),
        in_specs=[
            pl.BlockSpec(memory_space=pltpu.SMEM),
            pl.BlockSpec(memory_space=pltpu.VMEM),
            pl.BlockSpec(memory_space=pltpu.VMEM),
        ],
        out_specs=pl.BlockSpec(memory_space=pltpu.VMEM),
        cost_estimate=cost(7.0),
        compiler_params=pltpu.CompilerParams(vmem_limit_bytes=16 * MIB),
        name="path_masks",
    )(first, table, left)


def attend_tokens(tokens, rows, keys, values, levels, out_ref):
    chunk = 2 * ROWS if tokens < 3000 else ROWS

    def span(block):
        return pl.ds(pl.multiple_of(block * chunk, chunk), chunk)

    def score(block):
        return lax.dot_general(
            rows[span(block), :], keys[0:tokens, :], (((1,), (1,)), ((), ())),
            preferred_element_type=jnp.float32,
        )

    def weigh(scores):
        top = jnp.max(scores, axis=1, keepdims=True) * C2
        return top, jnp.exp2(scores * C2 - top).astype(jnp.bfloat16)

    def store(block, top, weights):
        summed = jnp.dot(weights, values[0:tokens, :], preferred_element_type=jnp.float32)
        total = summed[:, HD : 2 * HD]
        result = (summed[:, 0:HD] / total).astype(jnp.bfloat16)
        for part in range(chunk // ROWS):
            out_ref[block * (chunk // ROWS) + part, 0:ROWS, :] = result[part * ROWS : (part + 1) * ROWS]
        levels[span(block), :] = top + jnp.log2(total)

    def some_blocks(step, carry):
        first = step * TOGETHER
        scores, held = score(first), None
        for index in range(TOGETHER):
            following = score(first + index + 1) if index + 1 < TOGETHER else None
            top, weights = weigh(scores)
            if held is not None:
                store(*held)
            held, scores = (first + index, top, weights), following
        store(*held)
        return carry

    lax.fori_loop(0, RING * ROWS // chunk // TOGETHER, some_blocks, 0)


def attend_kernel(
    list_ref, used_ref, query_ref, ka_ref, va_ref, kb_ref, vb_ref, kc_ref, vc_ref, kd_ref, vd_ref,
    count_ref, out_ref, keys, values, rows, levels,
):
    token = lax.broadcasted_iota(jnp.int32, (PAGE, HD), 0)
    pool = ((ka_ref, va_ref), (kb_ref, vb_ref), (kc_ref, vc_ref), (kd_ref, vd_ref))
    filled = jnp.int32(0)
    for group, (key_ref, value_ref) in enumerate(pool):

        def some_pages(step, carry, group=group, key_ref=key_ref, value_ref=value_ref, filled=filled):
            for lane in range(UNROLL):
                page = list_ref[group * PAGES_DEV + step * UNROLL + lane]
                target = pl.ds(pl.multiple_of((filled + step * UNROLL + lane) * PAGE, PAGE), PAGE)
                keys[target, 0:HD] = key_ref[page]
                held = jnp.broadcast_to(count_ref[pl.ds(group * PAGES_DEV + page, 1), :], (PAGE, HD))
                keys[target, HD : 2 * HD] = jnp.where(token >= held, -BIG, 0.0).astype(jnp.bfloat16)
                values[target, 0:HD] = value_ref[page]
            return carry

        lax.fori_loop(0, (used_ref[group] + UNROLL - 1) // UNROLL, some_pages, 0)
        filled = filled + used_ref[group]
    place = lax.broadcasted_iota(jnp.int32, (CS, 16), 0) // 4
    spread = jnp.where(lax.broadcasted_iota(jnp.int32, (CS, 16), 1) == place, 1.0, 0.0).astype(jnp.bfloat16)
    for block in range(RING):
        hot = jnp.dot(spread, query_ref[block, ROWS : ROWS + 16, :], preferred_element_type=jnp.float32)
        hot = hot.astype(jnp.bfloat16)
        rows[block * ROWS : (block + 1) * ROWS, 0:HD] = query_ref[block, 0:ROWS, :]
        for head in range(HEADS):
            at = block * ROWS + head * CS
            rows[at : at + CS, HD : 2 * HD] = hot

    lower = -1
    for tokens in SIZES:

        @pl.when((filled * PAGE > lower) & (filled * PAGE <= tokens))
        def run(tokens=tokens):
            def one_blank(page, carry):
                target = pl.ds(pl.multiple_of(page * PAGE, PAGE), PAGE)
                keys[target, 0:HD] = jnp.zeros((PAGE, HD), jnp.bfloat16)
                keys[target, HD : 2 * HD] = jnp.full((PAGE, HD), -BIG, jnp.bfloat16)
                values[target, 0:HD] = jnp.zeros((PAGE, HD), jnp.bfloat16)
                return carry

            lax.fori_loop(filled, tokens // PAGE, one_blank, 0)
            values[0:tokens, HD : 2 * HD] = jnp.ones((tokens, HD), jnp.bfloat16)
            attend_tokens(tokens, rows, keys, values, levels, out_ref)

        lower = tokens
    diagonal = lax.broadcasted_iota(jnp.int32, (HD, HD), 0) == lax.broadcasted_iota(jnp.int32, (HD, HD), 1)
    for block in range(RING):
        level = levels[block * ROWS : (block + 1) * ROWS, :]
        lines = [
            jnp.sum(jnp.where(diagonal, level[half * HD : (half + 1) * HD], 0.0), axis=0, keepdims=True)
            for half in range(2)
        ]
        line = jnp.concatenate(lines, axis=0)
        high = line.astype(jnp.bfloat16).astype(jnp.float32)
        middle = (line - high).astype(jnp.bfloat16).astype(jnp.float32)
        low = line - high - middle
        tail = jnp.concatenate([high, middle, low, jnp.zeros((10, HD), jnp.float32)], axis=0)
        out_ref[block, ROWS : ROWS + 16, :] = tail.astype(jnp.bfloat16)


def attend(pages, used, query, pool, count):
    tokens = (GROUPS * PAGES_DEV + UNROLL) * PAGE
    vmem = pl.BlockSpec(memory_space=pltpu.VMEM)
    smem = pl.BlockSpec(memory_space=pltpu.SMEM)
    return pl.pallas_call(
        attend_kernel,
        out_shape=jax.ShapeDtypeStruct((RING, ROWS + 16, HD), jnp.bfloat16),
        in_specs=[smem, smem] + [vmem] * 10,
        out_specs=vmem,
        scratch_shapes=[
            pltpu.VMEM((tokens, 2 * HD), jnp.bfloat16),
            pltpu.VMEM((tokens, 2 * HD), jnp.bfloat16),
            pltpu.VMEM((RING * ROWS, 2 * HD), jnp.bfloat16),
            pltpu.VMEM((RING * ROWS, HD), jnp.float32),
        ],
        cost_estimate=cost(10.0),
        compiler_params=pltpu.CompilerParams(vmem_limit_bytes=30 * MIB),
        name="attend",
    )(pages, used, query, *pool, count)


def permit_kernel(finished_ref, allowed_ref, alive_ref):
    row = lax.broadcasted_iota(jnp.int32, (CS, HD), 0)
    column = lax.broadcasted_iota(jnp.int32, (CS, HD), 1)
    same = (row // 4 == column // 4) & (column <= row)
    alive = 1 - finished_ref[...]
    allowed_ref[...] = jnp.where(same, jnp.broadcast_to(alive, (CS, HD)), 0)
    own = jnp.where(row == column, jnp.broadcast_to(alive, (CS, HD)), 0)
    alive_ref[...] = jnp.broadcast_to(jnp.sum(own, axis=1, keepdims=True), (CS, HD)).astype(jnp.float32)


def permit(finished):
    vmem = pl.BlockSpec(memory_space=pltpu.VMEM)
    return pl.pallas_call(
        permit_kernel,
        out_shape=(jax.ShapeDtypeStruct((CS, HD), jnp.int32), jax.ShapeDtypeStruct((CS, HD), jnp.float32)),
        in_specs=[vmem],
        out_specs=(vmem, vmem),
        cost_estimate=cost(15.0),
        compiler_params=pltpu.CompilerParams(vmem_limit_bytes=2 * MIB),
        name="permit",
    )(finished)


def finish_kernel(
    parts_ref, query_ref, key_ref, value_ref, allowed_ref, alive_ref, weight_ref, out_ref
):
    width = out_ref.shape[2]
    diagonal = lax.broadcasted_iota(jnp.int32, (HD, HD), 0) == lax.broadcasted_iota(jnp.int32, (HD, HD), 1)
    levels = []
    for block in range(RING):
        tail = parts_ref[block, ROWS : ROWS + 16, :].astype(jnp.float32)
        line = tail[0:2] + tail[2:4] + tail[4:6]
        columns = [
            jnp.sum(jnp.where(diagonal, jnp.broadcast_to(line[half : half + 1], (HD, HD)), 0.0), axis=1, keepdims=True)
            for half in range(2)
        ]
        levels.append(jnp.concatenate(columns, axis=0))
    query = query_ref[0, 0:ROWS, :]
    scores = lax.dot_general(
        query, key_ref[...], (((1,), (1,)), ((), ())), preferred_element_type=jnp.float32
    )
    allowed = jnp.concatenate([allowed_ref[:, 0:CS]] * HEADS, axis=0) > 0
    scores = jnp.where(allowed, scores * C2, -BIG)
    own_top = jnp.max(scores, axis=1, keepdims=True)
    own = jnp.where(allowed, jnp.exp2(scores - own_top), 0.0)
    own_sum = jnp.dot(own.astype(jnp.bfloat16), value_ref[...], preferred_element_type=jnp.float32)
    best = own_top
    for level in levels:
        best = jnp.maximum(best, level)
    factor = jnp.exp2(own_top - best)
    total = factor * jnp.sum(own, axis=1, keepdims=True)
    summed = factor * own_sum
    for block in range(RING):
        factor = jnp.exp2(levels[block] - best)
        total = total + factor
        summed = summed + factor * parts_ref[block, 0:ROWS, :].astype(jnp.float32)
    result = (summed / total).astype(jnp.bfloat16)
    attended = jnp.concatenate([result[head * CS : (head + 1) * CS, :] for head in range(HEADS)], axis=1)

    for part in range(out_ref.shape[0]):
        columns = weight_ref[:, part * width : (part + 1) * width]
        terms = jnp.dot(attended, columns, preferred_element_type=jnp.float32)
        out_ref[part] = (terms * alive_ref[:, 0:1]).astype(jnp.bfloat16)


def finish(parts, query, keys, values, allowed, alive, weight):
    blocks = 8
    width = weight.shape[1] // blocks
    vmem = pl.BlockSpec(memory_space=pltpu.VMEM)
    return pl.pallas_call(
        finish_kernel,
        out_shape=jax.ShapeDtypeStruct((blocks, CS, width), jnp.bfloat16),
        in_specs=[vmem] * 7,
        out_specs=vmem,
        cost_estimate=cost(4.0),
        compiler_params=pltpu.CompilerParams(vmem_limit_bytes=12 * MIB),
        name="finish",
    )(parts, query, keys, values, allowed, alive, weight)


def body(
    queries, new_keys, new_values, pool_keys, pool_values, out_weight, page_table, prefix_len, parent, finished
):
    children, steps, width = queries.shape
    rows = children * steps
    nodes, path_pages = page_table.shape
    sent = prepare(parent, queries)
    gathered = lax.all_to_all(sent, "z", split_axis=0, concat_axis=0, tiled=True)

    def swap(values, axis):
        return [lax.ppermute(value, axis, [(0, 1), (1, 0)]) for value in values]

    kv = [pool_keys, pool_values]
    kv_far = swap(kv, "yh")
    near_keys, near_values, sent = lax.optimization_barrier((pool_keys, pool_values, sent))
    kv_core = swap([near_keys, near_values], "c")
    yh, z, core = lax.axis_index("yh"), lax.axis_index("z"), lax.axis_index("c")
    first = jnp.stack(
        [
            PAGES_DEV * ((a * RING + z) * 2 + b)
            for a, b in ((yh, core), (yh, 1 - core), (1 - yh, core), (1 - yh, 1 - core))
        ]
    ).astype(jnp.int32)
    table = page_table.T.reshape(nodes * path_pages // HD, HD)
    place = jnp.arange(path_pages, dtype=jnp.int32)
    left = jnp.clip(prefix_len[None, :] - PAGE * place[:, None], 0, PAGE).reshape(table.shape)
    count = path_masks(first, table, left)
    kv_far[0], kv_far[1], count = lax.optimization_barrier((kv_far[0], kv_far[1], count))
    kv_far_core = swap(kv_far, "c")
    taken = jnp.any(count[:, :nodes] > 0, axis=1).reshape(GROUPS, PAGES_DEV)
    order = jnp.arange(PAGES_DEV, dtype=jnp.int32)
    earlier = taken[:, None, :] & (order[None, None, :] < order[None, :, None])
    rank = jnp.sum(earlier.astype(jnp.int32), axis=2)
    chosen = taken[:, :, None] & (rank[:, :, None] == order[None, None, :])
    pages = jnp.sum(jnp.where(chosen, order[None, :, None], 0), axis=1).reshape(GROUPS * PAGES_DEV)
    used = jnp.sum(taken.astype(jnp.int32), axis=1)
    parts = attend(pages, used, gathered, kv + kv_core + kv_far + kv_far_core, count)
    line = jnp.pad(finished.reshape(1, rows), ((0, 0), (0, HD - rows)), constant_values=1)
    parts, line = lax.optimization_barrier((parts, line))
    allowed, alive = permit(line)
    parts = lax.all_to_all(parts, "z", split_axis=0, concat_axis=0, tiled=True)

    terms = finish(
        parts,
        sent,
        new_keys.reshape(rows, HD),
        new_values.reshape(rows, HD),
        allowed,
        alive,
        out_weight,
    )
    terms = lax.all_to_all(terms, ("yl", "x"), split_axis=0, concat_axis=0, tiled=True)
    return jnp.sum(terms.astype(jnp.float32), axis=0).reshape(children, steps, terms.shape[-1])


def solution(mesh):
    fine = Mesh(mesh.devices.reshape(2, RING, 2, 2, 4), ("yh", "z", "c", "yl", "x"))
    branch, tensor = ("yh", "z", "c"), ("yl", "x")
    placed = (
        P(branch, None, tensor),
        P(branch, None, tensor),
        P(branch, None, tensor),
        P(branch, None, tensor),
        P(branch, None, tensor),
        P(tensor, None),
        P(),
        P(),
        P(branch),
        P(branch, None),
    )
    return jax.shard_map(
        body, mesh=fine, in_specs=placed, out_specs=P(branch, None, tensor), check_vma=False
    )
```

```python
import functools

import jax
import jax.numpy as jnp
from jax import lax
from jax.experimental import pallas as pl
from jax.experimental.pallas import tpu as pltpu
from jax.sharding import Mesh, PartitionSpec as P

HD = 128
PAGE = 16
PAGES_DEV = 96
GROUPS = 4
RING = 8
ROWS = 256
HEADS = 8
CS = 32
UNROLL = 8
TOGETHER = 2
SIZES = (2304, 2560, 6144)
BIG = 2.0**100
C2 = HD**-0.5 * 1.4426950408889634
MIB = 1024 * 1024


def cost(microseconds):
    return pl.CostEstimate(flops=int(microseconds * 1.15e9), bytes_accessed=2**16, transcendentals=0)


def prepare_kernel(parent_ref, query_ref, out_ref, wide):
    child = lax.broadcasted_iota(jnp.int32, (16, HD), 0)
    lane = lax.broadcasted_iota(jnp.int32, (16, HD), 1)
    hot = jnp.zeros((16, HD), jnp.float32)
    for number in range(8):
        wide[number * 4 : number * 4 + 4, :] = query_ref[number].astype(jnp.float32)
        hot = jnp.where((child == number) & (lane == parent_ref[number]), 1.0, hot)
    hot = hot.astype(jnp.bfloat16)
    held = wide[...].astype(jnp.bfloat16)
    for copy in range(RING):
        for head in range(HEADS):
            out_ref[copy, head * CS : (head + 1) * CS, :] = held[:, head * HD : (head + 1) * HD]
        out_ref[copy, ROWS : ROWS + 16, :] = hot


def prepare(parent, queries):
    return pl.pallas_call(
        prepare_kernel,
        out_shape=jax.ShapeDtypeStruct((RING, ROWS + 16, HD), jnp.bfloat16),
        in_specs=[pl.BlockSpec(memory_space=pltpu.SMEM), pl.BlockSpec(memory_space=pltpu.VMEM)],
        out_specs=pl.BlockSpec(memory_space=pltpu.VMEM),
        scratch_shapes=[pltpu.VMEM((CS, HEADS * HD), jnp.float32)],
        cost_estimate=cost(1.0),
        compiler_params=pltpu.CompilerParams(vmem_limit_bytes=60 * MIB),
        name="prepare",
    )(parent, queries)


def mask_kernel(first_ref, table_ref, left_ref, count_ref):
    left = left_ref[...]
    for block in range(GROUPS):
        first = first_ref[block]

        def one_page(page, carry, block=block, first=first):
            hit = jnp.where(table_ref[...] == first + page, left, 0)
            count_ref[pl.ds(block * PAGES_DEV + page, 1), :] = jnp.sum(hit, axis=0, keepdims=True)
            return carry

        lax.fori_loop(0, PAGES_DEV, one_page, 0, unroll=8)
    part = count_ref[...]
    part = part + pltpu.roll(part, 64, 1)
    count_ref[...] = part + pltpu.roll(part, 32, 1)


def path_masks(first, table, left):
    return pl.pallas_call(
        mask_kernel,
        out_shape=jax.ShapeDtypeStruct((GROUPS * PAGES_DEV, HD), jnp.int32),
        in_specs=[
            pl.BlockSpec(memory_space=pltpu.SMEM),
            pl.BlockSpec(memory_space=pltpu.VMEM),
            pl.BlockSpec(memory_space=pltpu.VMEM),
        ],
        out_specs=pl.BlockSpec(memory_space=pltpu.VMEM),
        cost_estimate=cost(7.0),
        compiler_params=pltpu.CompilerParams(vmem_limit_bytes=16 * MIB),
        name="path_masks",
    )(first, table, left)


def attend_tokens(tokens, rows, keys, values, levels, out_ref):
    chunk = 2 * ROWS if tokens < 3000 else ROWS

    def span(block):
        return pl.ds(pl.multiple_of(block * chunk, chunk), chunk)

    def score(block):
        return lax.dot_general(
            rows[span(block), :], keys[0:tokens, :], (((1,), (1,)), ((), ())),
            preferred_element_type=jnp.float32,
        )

    def weigh(scores):
        top = jnp.max(scores, axis=1, keepdims=True) * C2
        return top, jnp.exp2(scores * C2 - top).astype(jnp.bfloat16)

    def store(block, top, weights):
        summed = jnp.dot(weights, values[0:tokens, :], preferred_element_type=jnp.float32)
        total = summed[:, HD : 2 * HD]
        result = (summed[:, 0:HD] / total).astype(jnp.bfloat16)
        for part in range(chunk // ROWS):
            out_ref[block * (chunk // ROWS) + part, 0:ROWS, :] = result[part * ROWS : (part + 1) * ROWS]
        levels[span(block), :] = top + jnp.log2(total)

    def some_blocks(step, carry):
        first = step * TOGETHER
        scores, held = score(first), None
        for index in range(TOGETHER):
            following = score(first + index + 1) if index + 1 < TOGETHER else None
            top, weights = weigh(scores)
            if held is not None:
                store(*held)
            held, scores = (first + index, top, weights), following
        store(*held)
        return carry

    lax.fori_loop(0, RING * ROWS // chunk // TOGETHER, some_blocks, 0)


def attend_kernel(
    list_ref, used_ref, query_ref, ka_ref, va_ref, kb_ref, vb_ref, kc_ref, vc_ref, kd_ref, vd_ref,
    count_ref, out_ref, keys, values, rows, levels,
):
    token = lax.broadcasted_iota(jnp.int32, (PAGE, HD), 0)
    pool = ((ka_ref, va_ref), (kb_ref, vb_ref), (kc_ref, vc_ref), (kd_ref, vd_ref))
    filled = jnp.int32(0)
    for group, (key_ref, value_ref) in enumerate(pool):

        def some_pages(step, carry, group=group, key_ref=key_ref, value_ref=value_ref, filled=filled):
            for lane in range(UNROLL):
                page = list_ref[group * PAGES_DEV + step * UNROLL + lane]
                target = pl.ds(pl.multiple_of((filled + step * UNROLL + lane) * PAGE, PAGE), PAGE)
                keys[target, 0:HD] = key_ref[page]
                held = jnp.broadcast_to(count_ref[pl.ds(group * PAGES_DEV + page, 1), :], (PAGE, HD))
                keys[target, HD : 2 * HD] = jnp.where(token >= held, -BIG, 0.0).astype(jnp.bfloat16)
                values[target, 0:HD] = value_ref[page]
            return carry

        lax.fori_loop(0, (used_ref[group] + UNROLL - 1) // UNROLL, some_pages, 0)
        filled = filled + used_ref[group]
    place = lax.broadcasted_iota(jnp.int32, (CS, 16), 0) // 4
    spread = jnp.where(lax.broadcasted_iota(jnp.int32, (CS, 16), 1) == place, 1.0, 0.0).astype(jnp.bfloat16)
    for block in range(RING):
        hot = jnp.dot(spread, query_ref[block, ROWS : ROWS + 16, :], preferred_element_type=jnp.float32)
        hot = hot.astype(jnp.bfloat16)
        rows[block * ROWS : (block + 1) * ROWS, 0:HD] = query_ref[block, 0:ROWS, :]
        for head in range(HEADS):
            at = block * ROWS + head * CS
            rows[at : at + CS, HD : 2 * HD] = hot

    lower = -1
    for tokens in SIZES:

        @pl.when((filled * PAGE > lower) & (filled * PAGE <= tokens))
        def run(tokens=tokens):
            def one_blank(page, carry):
                target = pl.ds(pl.multiple_of(page * PAGE, PAGE), PAGE)
                keys[target, 0:HD] = jnp.zeros((PAGE, HD), jnp.bfloat16)
                keys[target, HD : 2 * HD] = jnp.full((PAGE, HD), -BIG, jnp.bfloat16)
                values[target, 0:HD] = jnp.zeros((PAGE, HD), jnp.bfloat16)
                return carry

            lax.fori_loop(filled, tokens // PAGE, one_blank, 0)
            values[0:tokens, HD : 2 * HD] = jnp.ones((tokens, HD), jnp.bfloat16)
            attend_tokens(tokens, rows, keys, values, levels, out_ref)

        lower = tokens
    diagonal = lax.broadcasted_iota(jnp.int32, (HD, HD), 0) == lax.broadcasted_iota(jnp.int32, (HD, HD), 1)
    for block in range(RING):
        level = levels[block * ROWS : (block + 1) * ROWS, :]
        lines = [
            jnp.sum(jnp.where(diagonal, level[half * HD : (half + 1) * HD], 0.0), axis=0, keepdims=True)
            for half in range(2)
        ]
        line = jnp.concatenate(lines, axis=0)
        high = line.astype(jnp.bfloat16).astype(jnp.float32)
        middle = (line - high).astype(jnp.bfloat16).astype(jnp.float32)
        low = line - high - middle
        tail = jnp.concatenate([high, middle, low, jnp.zeros((10, HD), jnp.float32)], axis=0)
        out_ref[block, ROWS : ROWS + 16, :] = tail.astype(jnp.bfloat16)


def attend(pages, used, query, pool, count):
    tokens = (GROUPS * PAGES_DEV + UNROLL) * PAGE
    vmem = pl.BlockSpec(memory_space=pltpu.VMEM)
    smem = pl.BlockSpec(memory_space=pltpu.SMEM)
    return pl.pallas_call(
        attend_kernel,
        out_shape=jax.ShapeDtypeStruct((RING, ROWS + 16, HD), jnp.bfloat16),
        in_specs=[smem, smem] + [vmem] * 10,
        out_specs=vmem,
        scratch_shapes=[
            pltpu.VMEM((tokens, 2 * HD), jnp.bfloat16),
            pltpu.VMEM((tokens, 2 * HD), jnp.bfloat16),
            pltpu.VMEM((RING * ROWS, 2 * HD), jnp.bfloat16),
            pltpu.VMEM((RING * ROWS, HD), jnp.float32),
        ],
        cost_estimate=cost(10.0),
        compiler_params=pltpu.CompilerParams(vmem_limit_bytes=30 * MIB),
        name="attend",
    )(pages, used, query, *pool, count)


def permit_kernel(finished_ref, allowed_ref, alive_ref):
    row = lax.broadcasted_iota(jnp.int32, (CS, HD), 0)
    column = lax.broadcasted_iota(jnp.int32, (CS, HD), 1)
    same = (row // 4 == column // 4) & (column <= row)
    alive = 1 - finished_ref[...]
    allowed_ref[...] = jnp.where(same, jnp.broadcast_to(alive, (CS, HD)), 0)
    own = jnp.where(row == column, jnp.broadcast_to(alive, (CS, HD)), 0)
    alive_ref[...] = jnp.broadcast_to(jnp.sum(own, axis=1, keepdims=True), (CS, HD)).astype(jnp.float32)


def permit(finished):
    vmem = pl.BlockSpec(memory_space=pltpu.VMEM)
    return pl.pallas_call(
        permit_kernel,
        out_shape=(jax.ShapeDtypeStruct((CS, HD), jnp.int32), jax.ShapeDtypeStruct((CS, HD), jnp.float32)),
        in_specs=[vmem],
        out_specs=(vmem, vmem),
        cost_estimate=cost(15.0),
        compiler_params=pltpu.CompilerParams(vmem_limit_bytes=2 * MIB),
        name="permit",
    )(finished)


def merge_kernel(parts_ref, query_ref, key_ref, value_ref, allowed_ref, out_ref):
    diagonal = lax.broadcasted_iota(jnp.int32, (HD, HD), 0) == lax.broadcasted_iota(jnp.int32, (HD, HD), 1)
    levels = []
    for block in range(RING):
        tail = parts_ref[block, ROWS : ROWS + 16, :].astype(jnp.float32)
        line = tail[0:2] + tail[2:4] + tail[4:6]
        columns = [
            jnp.sum(jnp.where(diagonal, jnp.broadcast_to(line[half : half + 1], (HD, HD)), 0.0), axis=1, keepdims=True)
            for half in range(2)
        ]
        levels.append(jnp.concatenate(columns, axis=0))
    query = query_ref[0, 0:ROWS, :]
    scores = lax.dot_general(
        query, key_ref[...], (((1,), (1,)), ((), ())), preferred_element_type=jnp.float32
    )
    allowed = jnp.concatenate([allowed_ref[:, 0:CS]] * HEADS, axis=0) > 0
    scores = jnp.where(allowed, scores * C2, -BIG)
    own_top = jnp.max(scores, axis=1, keepdims=True)
    own = jnp.where(allowed, jnp.exp2(scores - own_top), 0.0)
    own_sum = jnp.dot(own.astype(jnp.bfloat16), value_ref[...], preferred_element_type=jnp.float32)
    best = own_top
    for level in levels:
        best = jnp.maximum(best, level)
    factor = jnp.exp2(own_top - best)
    total = factor * jnp.sum(own, axis=1, keepdims=True)
    summed = factor * own_sum
    for block in range(RING):
        factor = jnp.exp2(levels[block] - best)
        total = total + factor
        summed = summed + factor * parts_ref[block, 0:ROWS, :].astype(jnp.float32)
    result = (summed / total).astype(jnp.bfloat16)
    for head in range(HEADS):
        out_ref[:, head * HD : (head + 1) * HD] = result[head * CS : (head + 1) * CS, :]


def merge(parts, query, keys, values, allowed):
    vmem = pl.BlockSpec(memory_space=pltpu.VMEM)
    return pl.pallas_call(
        merge_kernel,
        out_shape=jax.ShapeDtypeStruct((CS, HEADS * HD), jnp.bfloat16),
        in_specs=[vmem] * 5,
        out_specs=vmem,
        cost_estimate=cost(4.0),
        compiler_params=pltpu.CompilerParams(vmem_limit_bytes=6 * MIB),
        name="merge",
    )(parts, query, keys, values, allowed)


def project_kernel(attended_ref, alive_ref, weight_ref, out_ref):
    width = out_ref.shape[2]
    for part in range(out_ref.shape[0]):
        columns = weight_ref[:, part * width : (part + 1) * width]
        terms = jnp.dot(attended_ref[...], columns, preferred_element_type=jnp.float32)
        out_ref[part] = (terms * alive_ref[:, 0:1]).astype(jnp.bfloat16)


def project(attended, alive, weight):
    blocks = 8
    width = weight.shape[1] // blocks
    vmem = pl.BlockSpec(memory_space=pltpu.VMEM)
    return pl.pallas_call(
        project_kernel,
        out_shape=jax.ShapeDtypeStruct((blocks, CS, width), jnp.bfloat16),
        in_specs=[vmem] * 3,
        out_specs=vmem,
        cost_estimate=cost(2.0),
        compiler_params=pltpu.CompilerParams(vmem_limit_bytes=6 * MIB),
        name="project",
    )(attended, alive, weight)


def body(
    queries, new_keys, new_values, pool_keys, pool_values, out_weight, page_table, prefix_len, parent, finished
):
    children, steps, width = queries.shape
    rows = children * steps
    nodes, path_pages = page_table.shape
    sent = prepare(parent, queries)
    gathered = lax.all_to_all(sent, "z", split_axis=0, concat_axis=0, tiled=True)

    def swap(values, axis):
        return [lax.ppermute(value, axis, [(0, 1), (1, 0)]) for value in values]

    kv = [pool_keys, pool_values]
    kv_far = swap(kv, "yh")
    near_keys, near_values, sent = lax.optimization_barrier((pool_keys, pool_values, sent))
    kv_core = swap([near_keys, near_values], "c")
    yh, z, core = lax.axis_index("yh"), lax.axis_index("z"), lax.axis_index("c")
    first = jnp.stack(
        [
            PAGES_DEV * ((a * RING + z) * 2 + b)
            for a, b in ((yh, core), (yh, 1 - core), (1 - yh, core), (1 - yh, 1 - core))
        ]
    ).astype(jnp.int32)
    table = page_table.T.reshape(nodes * path_pages // HD, HD)
    place = jnp.arange(path_pages, dtype=jnp.int32)
    left = jnp.clip(prefix_len[None, :] - PAGE * place[:, None], 0, PAGE).reshape(table.shape)
    count = path_masks(first, table, left)
    kv_far[0], kv_far[1], count = lax.optimization_barrier((kv_far[0], kv_far[1], count))
    kv_far_core = swap(kv_far, "c")
    taken = jnp.any(count[:, :nodes] > 0, axis=1).reshape(GROUPS, PAGES_DEV)
    order = jnp.arange(PAGES_DEV, dtype=jnp.int32)
    earlier = taken[:, None, :] & (order[None, None, :] < order[None, :, None])
    rank = jnp.sum(earlier.astype(jnp.int32), axis=2)
    chosen = taken[:, :, None] & (rank[:, :, None] == order[None, None, :])
    pages = jnp.sum(jnp.where(chosen, order[None, :, None], 0), axis=1).reshape(GROUPS * PAGES_DEV)
    used = jnp.sum(taken.astype(jnp.int32), axis=1)
    parts = attend(pages, used, gathered, kv + kv_core + kv_far + kv_far_core, count)
    line = jnp.pad(finished.reshape(1, rows), ((0, 0), (0, HD - rows)), constant_values=1)
    parts, line = lax.optimization_barrier((parts, line))
    allowed, alive = permit(line)
    parts = lax.all_to_all(parts, "z", split_axis=0, concat_axis=0, tiled=True)

    attended = merge(parts, sent, new_keys.reshape(rows, HD), new_values.reshape(rows, HD), allowed)
    terms = project(attended, alive, out_weight)
    terms = lax.all_to_all(terms, ("yl", "x"), split_axis=0, concat_axis=0, tiled=True)
    return jnp.sum(terms.astype(jnp.float32), axis=0).reshape(children, steps, terms.shape[-1])


def solution(mesh):
    fine = Mesh(mesh.devices.reshape(2, RING, 2, 2, 4), ("yh", "z", "c", "yl", "x"))
    branch, tensor = ("yh", "z", "c"), ("yl", "x")
    placed = (
        P(branch, None, tensor),
        P(branch, None, tensor),
        P(branch, None, tensor),
        P(branch, None, tensor),
        P(branch, None, tensor),
        P(tensor, None),
        P(),
        P(),
        P(branch),
        P(branch, None),
    )
    return jax.shard_map(
        body, mesh=fine, in_specs=placed, out_specs=P(branch, None, tensor), check_vma=False
    )
```
